32 devices in a mesh: req: 8 (over z, x), tp: 4 (over y, core).
Axes of the slice: x: 2, y: 2, z: 4, core: 2. Of those that a mesh axis runs over, the one named last changes fastest.
Arguments:
- hidden_in: bfloat16 [16, 512, 1280], P('req'), may hold values from -6 to 6
- lengths: int32 [16], P('req'), may hold values from 128 to 512, as said below
- attn_gain: float32 [1280], replicated, may hold values from 0.1 to 1.9
- mlp_gain: float32 [1280], replicated, may hold values from 0.1 to 1.9
- q_master: float32 [1280, 1280], P(('req', 'tp')), may hold values from -1 to 1
- k_master: float32 [1280, 320], P(('req', 'tp')), may hold values from -1 to 1
- trainer_value_weight: float32 [1280, 320], P(('req', 'tp')), may hold values from -0.15625 to 0.15625
- o_master: float32 [1280, 1280], P(('req', 'tp')), may hold values from -0.15625 to 0.15625
- gate_master: float32 [1280, 3584], P(('req', 'tp')), may hold values from -0.15625 to 0.15625
- up_master: float32 [1280, 3584], P(('req', 'tp')), may hold values from -0.15625 to 0.15625
- down_master: float32 [3584, 1280], P(('req', 'tp')), may hold values from -0.09375 to 0.09375
Outputs:
- hidden_out: bfloat16 [16, 512, 1280], P('req')
- kv_cache: bfloat16 [16, 512, 640], P('req')
The draws below stay inside these ranges and needn't reach their ends.
Inputs may be any that keep to these rules, and one draw needn't show every extreme that they name: `lengths`: each prompt has at least a quarter of 512 real tokens; in every draw some prompt has exactly 512.
All inputs are finite; a program needn't handle non-finite values.
Results may differ from the reference program's by a relative error of at most 0.012.
Values may be sent and summed in bfloat16 or wider, within the bound.
A program may use at most 192 MiB of HBM per device.

```python
import math
import jax
import jax.numpy as jnp
from jax import lax

MODEL_DIM = 1280
FF = 3584
QUERY_HEADS = 20
KEY_VALUE_HEADS = 5
HEAD_DIM = 64
PROMPT_LENGTH = 512
PROMPTS = 16
N_TP = 4


def draw_lengths(key, part):
    base_len = jax.random.randint(jax.random.fold_in(key, 11), (PROMPTS,), PROMPT_LENGTH // 4, PROMPT_LENGTH + 1)
    chosen = jax.random.randint(jax.random.fold_in(key, 12), (), 0, PROMPTS)
    return jnp.where(jnp.arange(PROMPTS) == chosen, PROMPT_LENGTH, base_len).astype(jnp.int32)


def unsharded_weight(key, salt, columns):
    raw = jax.random.normal(jax.random.fold_in(key, salt), (MODEL_DIM, columns), jnp.float32)
    return jnp.clip(raw, -6.0, 6.0) / math.sqrt(MODEL_DIM)


def draw_q_master(key, part):
    weight_table = unsharded_weight(key, 31, QUERY_HEADS * HEAD_DIM)
    return weight_table


def draw_k_master(key, part):
    weight_table = unsharded_weight(key, 32, KEY_VALUE_HEADS * HEAD_DIM)
    return weight_table


def draw_hidden_in(key, part):
    rows = jnp.clip(jax.random.normal(jax.random.fold_in(key, 33), (PROMPTS, PROMPT_LENGTH, MODEL_DIM), jnp.float32), -6.0, 6.0)
    return rows.astype(jnp.bfloat16)


def block_scale(rng, extent, shards, low, high):
    loudness, own = 1.0, jax.random.fold_in(rng, 6)
    for dim, blocks in shards:
        draws = jnp.exp(jax.random.uniform(jax.random.fold_in(own, dim), (blocks,), jnp.float32, low / len(shards), high / len(shards)))
        loudness = loudness * jnp.repeat(draws, extent[dim] // blocks).reshape([-1 if axis == dim else 1 for axis in range(len(extent))])
    return loudness


def gaussian(own_key, shape, scale, bound, split=(), kind=jnp.bfloat16):
    factor_of = block_scale(own_key, shape, split, -0.22, 0.18) if split else 1.0
    entries = jax.random.normal(own_key, shape, jnp.float32) * scale * factor_of
    return jnp.minimum(jnp.maximum(entries, -bound), bound).astype(kind)


def setup_inputs(seed: int = 0) -> dict:
    key_of = jax.random.split(jax.random.key(seed), 12)
    return {
        "hidden_in": draw_hidden_in(jax.random.fold_in(key_of[11], 71), 0),
        "lengths": draw_lengths(jax.random.fold_in(key_of[11], 71), 0),
        "attn_gain": jnp.clip(1.0 + 0.18 * jax.random.normal(key_of[2], (MODEL_DIM,), jnp.float32), 0.1, 1.9),
        "mlp_gain": jnp.clip(1.0 + 0.18 * jax.random.normal(key_of[3], (MODEL_DIM,), jnp.float32), 0.1, 1.9),
        "q_master": draw_q_master(jax.random.fold_in(key_of[11], 71), 0),
        "k_master": draw_k_master(jax.random.fold_in(key_of[11], 71), 0),
        "trainer_value_weight": gaussian(key_of[6], (MODEL_DIM, KEY_VALUE_HEADS * HEAD_DIM), MODEL_DIM ** -0.5, 0.15625, ((0, 32),), jnp.float32),
        "o_master": gaussian(key_of[7], (QUERY_HEADS * HEAD_DIM, MODEL_DIM), (QUERY_HEADS * HEAD_DIM) ** -0.5, 0.15625, ((0, 32),), jnp.float32),
        "gate_master": gaussian(key_of[8], (MODEL_DIM, FF), MODEL_DIM ** -0.5, 0.15625, ((0, 32),), jnp.float32),
        "up_master": gaussian(key_of[9], (MODEL_DIM, FF), MODEL_DIM ** -0.5, 0.15625, ((0, 32),), jnp.float32),
        "down_master": gaussian(key_of[10], (FF, MODEL_DIM), FF ** -0.5, 0.09375, ((0, 32),), jnp.float32),
    }


def rms_norm(field, gain_vec):
    scale = lax.rsqrt(lax.optimization_barrier(jnp.mean(field * field, axis=-1, keepdims=True)) + 1e-05)
    return (field * scale * gain_vec).astype(jnp.bfloat16)

def rope_tables(sequence_length, head_size):
    half_width = head_size // 2
    positions = jnp.arange(sequence_length, dtype=jnp.float32)[:, None]
    frequency = jnp.exp(-math.log(10000.0) * (2.0 * jnp.arange(half_width, dtype=jnp.float32) / head_size))
    angles = positions * frequency[None, :]
    return (jnp.cos(angles), jnp.sin(angles))

def rotate(field, cosine_table, sine_table):
    half_width = field.shape[-1] // 2
    first_half = field[..., :half_width]
    second_half = field[..., half_width:]
    cos_b = cosine_table[:, None, :]
    sin_b = sine_table[:, None, :]
    return jnp.concatenate([first_half * cos_b - second_half * sin_b, second_half * cos_b + first_half * sin_b], axis=-1)

def block_sum(left, weight_rows):
    row_count, inner = left.shape
    split_left = left.reshape(row_count, N_TP, inner // N_TP).astype(jnp.float32)
    split_right = weight_rows.reshape(N_TP, inner // N_TP, weight_rows.shape[1]).astype(jnp.float32)
    partial_value = jnp.einsum('snk,nkd->nsd', split_left, split_right)
    rounded = lax.optimization_barrier(partial_value.astype(jnp.bfloat16))
    return lax.optimization_barrier(jnp.sum(rounded.astype(jnp.float32), axis=0))

def reference(hidden_in, lengths, attn_gain, mlp_gain, q_master, k_master, trainer_value_weight, o_master, gate_master, up_master, down_master):
    q_w = q_master.astype(jnp.bfloat16)
    key_matrix = k_master.astype(jnp.bfloat16)
    value_matrix = trainer_value_weight.astype(jnp.bfloat16)
    o_w = o_master.astype(jnp.bfloat16)
    gate_w = gate_master.astype(jnp.bfloat16)
    up_w = up_master.astype(jnp.bfloat16)
    down_w = down_master.astype(jnp.bfloat16)
    cosine_table, sine_table = rope_tables(PROMPT_LENGTH, HEAD_DIM)
    group_width = QUERY_HEADS // KEY_VALUE_HEADS

    def one_prompt(prompt_item):
        field, length = prompt_item
        rows_f = field.astype(jnp.float32)
        normalized_input = rms_norm(rows_f, attn_gain)
        queries = jnp.dot(normalized_input, q_w, preferred_element_type=jnp.float32).reshape(PROMPT_LENGTH, QUERY_HEADS, HEAD_DIM)
        key_rows = jnp.dot(normalized_input, key_matrix, preferred_element_type=jnp.float32).reshape(PROMPT_LENGTH, KEY_VALUE_HEADS, HEAD_DIM)
        value_rows = jnp.dot(normalized_input, value_matrix, preferred_element_type=jnp.float32).reshape(PROMPT_LENGTH, KEY_VALUE_HEADS, HEAD_DIM)
        q_rot = rotate(queries, cosine_table, sine_table).astype(jnp.bfloat16)
        rotated_keys = rotate(key_rows, cosine_table, sine_table).astype(jnp.bfloat16)
        value_halves = value_rows.astype(jnp.bfloat16)
        cache_entries = jnp.concatenate([rotated_keys.reshape(PROMPT_LENGTH, KEY_VALUE_HEADS * HEAD_DIM), value_halves.reshape(PROMPT_LENGTH, KEY_VALUE_HEADS * HEAD_DIM)], axis=1)
        k_all = jnp.repeat(rotated_keys, group_width, axis=1).astype(jnp.float32)
        v_all = jnp.repeat(value_halves, group_width, axis=1).astype(jnp.float32)
        scores = jnp.einsum('qhd,khd->hqk', q_rot.astype(jnp.float32), k_all) / math.sqrt(HEAD_DIM)
        row_index = jnp.arange(PROMPT_LENGTH, dtype=jnp.int32)[:, None]
        col_index = jnp.arange(PROMPT_LENGTH, dtype=jnp.int32)[None, :]
        allowed = (col_index <= row_index) & (col_index < length)
        scores = jnp.where(allowed[None], scores, -1e+30)
        highest = lax.optimization_barrier(jnp.max(scores, axis=-1, keepdims=True))
        expo = jnp.exp(scores - highest)
        weight_table = (expo / lax.optimization_barrier(jnp.sum(expo, axis=-1, keepdims=True))).astype(jnp.bfloat16)
        attended = jnp.einsum('hqk,khd->qhd', weight_table.astype(jnp.float32), v_all).astype(jnp.bfloat16).reshape(PROMPT_LENGTH, QUERY_HEADS * HEAD_DIM)
        middle = rows_f + block_sum(attended, o_w)
        normed2 = rms_norm(middle, mlp_gain)
        gate_val = jnp.dot(normed2, gate_w, preferred_element_type=jnp.float32)
        up_val = jnp.dot(normed2, up_w, preferred_element_type=jnp.float32)
        hidden_ff = (jax.nn.silu(gate_val) * up_val).astype(jnp.bfloat16)
        result = (middle + block_sum(hidden_ff, down_w)).astype(jnp.bfloat16)
        return (result, cache_entries)
    hidden_out, kv_cache = lax.map(one_prompt, (hidden_in, lengths))
    return (hidden_out, kv_cache)
```

```python
import math

import jax
import jax.numpy as jnp
from jax import lax
from jax.sharding import PartitionSpec as P

QUERY_HEADS = 20
KEY_VALUE_HEADS = 5
HEAD_DIM = 64


def rms_norm(field, gain_vec):
    scale = lax.rsqrt(jnp.mean(field * field, axis=-1, keepdims=True) + 1e-05)
    return (field * scale * gain_vec).astype(jnp.bfloat16)


def rope_tables(sequence_length, head_size):
    half_width = head_size // 2
    positions = jnp.arange(sequence_length, dtype=jnp.float32)[:, None]
    frequency = jnp.exp(
        -math.log(10000.0) * (2.0 * jnp.arange(half_width, dtype=jnp.float32) / head_size)
    )
    angles = positions * frequency[None, :]
    return (jnp.cos(angles), jnp.sin(angles))


def rotate(field, cosine_table, sine_table):
    half_width = field.shape[-1] // 2
    first_half = field[..., :half_width]
    second_half = field[..., half_width:]
    cos_b = cosine_table[:, None, :]
    sin_b = sine_table[:, None, :]
    return jnp.concatenate(
        [first_half * cos_b - second_half * sin_b, second_half * cos_b + first_half * sin_b],
        axis=-1,
    )


def local(
    hidden_in,
    lengths,
    attn_gain,
    mlp_gain,
    q_master,
    k_master,
    trainer_value_weight,
    o_master,
    gate_master,
    up_master,
    down_master,
):
    tp_count = lax.axis_size("tp")
    req_count = lax.axis_size("req")
    tensor_shard_index = lax.axis_index("tp")
    half = jnp.bfloat16
    shard_rows = q_master.shape[0]
    q_cols = q_master.shape[1] // tp_count
    kv_cols = k_master.shape[1]
    ff_cols = gate_master.shape[1] // tp_count
    down_rows = down_master.shape[0]

    q_parts = q_master.reshape(shard_rows, tp_count, q_cols).transpose(1, 0, 2)
    kv_parts = jnp.broadcast_to(
        jnp.concatenate([k_master, trainer_value_weight], axis=1)[None],
        (tp_count, shard_rows, 2 * kv_cols),
    )
    first_pack = jnp.concatenate([q_parts, kv_parts], axis=2).astype(half)
    first_pack = first_pack.reshape(tp_count * shard_rows, q_cols + 2 * kv_cols)
    first_pack = lax.all_to_all(first_pack, "tp", 0, 0, tiled=True)
    first_full = lax.all_gather(first_pack, "req", axis=0, tiled=True)

    def ff_parts(master):
        return (
            master.astype(half)
            .reshape(shard_rows, req_count, tp_count, down_rows)
            .transpose(2, 0, 1, 3)
            .reshape(tp_count * shard_rows, ff_cols)
        )

    second_pack = jnp.concatenate([ff_parts(gate_master), ff_parts(up_master)], axis=1)
    second_pack = lax.all_to_all(second_pack, "tp", 0, 0, tiled=True)
    o_full = lax.all_gather(o_master.astype(half), ("req", "tp"), axis=0, tiled=True)
    second_full = lax.all_gather(second_pack, "req", axis=0, tiled=True)
    down_weight = lax.all_gather(down_master.astype(half), "req", axis=0, tiled=True)

    query_weight = first_full[:, :q_cols]
    key_weight = first_full[:, q_cols : q_cols + kv_cols]
    value_weight = first_full[:, q_cols + kv_cols :]
    gate_weight = second_full[:, :ff_cols]
    up_weight = second_full[:, ff_cols:]
    prompt_batch, sequence_length, model_width = hidden_in.shape
    tok_rows = prompt_batch * sequence_length
    flat_rows = hidden_in.reshape(tok_rows, model_width).astype(jnp.float32)
    normalized_input = rms_norm(flat_rows, attn_gain)
    local_heads = query_weight.shape[1] // HEAD_DIM
    queries = jnp.dot(normalized_input, query_weight, preferred_element_type=jnp.float32).reshape(
        prompt_batch, sequence_length, local_heads, HEAD_DIM
    )
    key_rows = jnp.dot(normalized_input, key_weight, preferred_element_type=jnp.float32).reshape(
        prompt_batch, sequence_length, KEY_VALUE_HEADS, HEAD_DIM
    )
    value_rows = jnp.dot(
        normalized_input, value_weight, preferred_element_type=jnp.float32
    ).reshape(prompt_batch, sequence_length, KEY_VALUE_HEADS, HEAD_DIM)
    cosine_table, sine_table = rope_tables(sequence_length, HEAD_DIM)
    q_rot = rotate(queries, cosine_table, sine_table).astype(jnp.bfloat16)
    rotated_keys = rotate(key_rows, cosine_table, sine_table).astype(jnp.bfloat16)
    value_halves = value_rows.astype(jnp.bfloat16)
    kv_cache = jnp.concatenate(
        [
            rotated_keys.reshape(prompt_batch, sequence_length, KEY_VALUE_HEADS * HEAD_DIM),
            value_halves.reshape(prompt_batch, sequence_length, KEY_VALUE_HEADS * HEAD_DIM),
        ],
        axis=2,
    )
    owner_shards = (
        tensor_shard_index * local_heads + jnp.arange(local_heads, dtype=jnp.int32)
    ) // (QUERY_HEADS // KEY_VALUE_HEADS)
    selector_mask = (
        owner_shards[:, None] == jnp.arange(KEY_VALUE_HEADS, dtype=jnp.int32)[None, :]
    ).astype(jnp.bfloat16)
    k_local = jnp.einsum(
        "pshd,gh->psgd", rotated_keys, selector_mask, preferred_element_type=jnp.float32
    ).astype(jnp.bfloat16)
    v_local = jnp.einsum(
        "pshd,gh->psgd", value_halves, selector_mask, preferred_element_type=jnp.float32
    ).astype(jnp.bfloat16)
    scores = jnp.einsum(
        "pqhd,pkhd->phqk", q_rot, k_local, preferred_element_type=jnp.float32
    ) / math.sqrt(HEAD_DIM)
    row_index = jnp.arange(sequence_length, dtype=jnp.int32)[:, None]
    col_index = jnp.arange(sequence_length, dtype=jnp.int32)[None, :]
    allowed = (col_index <= row_index)[None, None] & (
        col_index[None, None] < lengths[:, None, None, None]
    )
    scores = jnp.where(allowed, scores, -1e30)
    highest = jnp.max(scores, axis=-1, keepdims=True)
    expo = jnp.exp(scores - highest)
    weight_table = (expo / jnp.sum(expo, axis=-1, keepdims=True)).astype(jnp.bfloat16)
    attended = (
        jnp.einsum("phqk,pkhd->pqhd", weight_table, v_local, preferred_element_type=jnp.float32)
        .astype(jnp.bfloat16)
        .reshape(tok_rows, local_heads * HEAD_DIM)
    )
    own_rows = tok_rows // tp_count
    attended_rows = lax.all_to_all(attended, "tp", 0, 1, tiled=True)
    own_hidden = lax.dynamic_slice_in_dim(flat_rows, tensor_shard_index * own_rows, own_rows, 0)
    middle = own_hidden + jnp.dot(attended_rows, o_full, preferred_element_type=jnp.float32)
    normed_rows = lax.all_gather(rms_norm(middle, mlp_gain), "tp", axis=0, tiled=True)
    gate_val = jnp.dot(normed_rows, gate_weight, preferred_element_type=jnp.float32)
    up_val = jnp.dot(normed_rows, up_weight, preferred_element_type=jnp.float32)
    hidden_ff = (jax.nn.silu(gate_val) * up_val).astype(jnp.bfloat16)
    ffn_rows = lax.psum_scatter(
        jnp.dot(hidden_ff, down_weight, preferred_element_type=jnp.float32).astype(jnp.bfloat16),
        "tp",
        scatter_dimension=0,
        tiled=True,
    ).astype(jnp.float32)
    result = lax.all_gather((middle + ffn_rows).astype(jnp.bfloat16), "tp", axis=0, tiled=True)
    return (result.reshape(prompt_batch, sequence_length, model_width), kv_cache)


def solution(mesh):
    placed = (
        P("req", None, None),
        P("req"),
        P(),
        P(),
        P(("req", "tp"), None),
        P(("req", "tp"), None),
        P(("req", "tp"), None),
        P(("req", "tp"), None),
        P(("req", "tp"), None),
        P(("req", "tp"), None),
        P(("req", "tp"), None),
    )
    return jax.shard_map(
        local,
        mesh=mesh,
        in_specs=placed,
        out_specs=(P("req", None, None), P("req", None, None)),
        check_vma=False,
    )
```

```python
import math

import jax
import jax.numpy as jnp
from jax import lax
from jax.sharding import PartitionSpec as P

QUERY_HEADS = 20
KEY_VALUE_HEADS = 5
HEAD_DIM = 64


def rms_norm(field, gain_vec):
    scale = lax.rsqrt(jnp.mean(field * field, axis=-1, keepdims=True) + 1e-05)
    return (field * scale * gain_vec).astype(jnp.bfloat16)


def rope_tables(sequence_length, head_size):
    half_width = head_size // 2
    positions = jnp.arange(sequence_length, dtype=jnp.float32)[:, None]
    frequency = jnp.exp(
        -math.log(10000.0) * (2.0 * jnp.arange(half_width, dtype=jnp.float32) / head_size)
    )
    angles = positions * frequency[None, :]
    return (jnp.cos(angles), jnp.sin(angles))


def rotate(field, cosine_table, sine_table):
    half_width = field.shape[-1] // 2
    first_half = field[..., :half_width]
    second_half = field[..., half_width:]
    cos_b = cosine_table[:, None, :]
    sin_b = sine_table[:, None, :]
    return jnp.concatenate(
        [first_half * cos_b - second_half * sin_b, second_half * cos_b + first_half * sin_b],
        axis=-1,
    )


def tp_permute(field, flip):
    return lax.ppermute(field, "tp", [(s, s ^ flip) for s in range(lax.axis_size("tp"))])


def gather_req(shard):
    count = lax.axis_size("req")
    inner = 2
    outer = count // inner
    me = lax.axis_index("req")
    far, near = me // inner, me % inner
    out = jnp.zeros((outer, inner) + shard.shape, shard.dtype)
    zeros = (0,) * shard.ndim
    for step in range(outer):
        held = shard
        if step:
            pairs = [(r, (r + step * inner) % count) for r in range(count)]
            held = lax.ppermute(shard, "req", pairs)
        other = lax.ppermute(held, "req", [(r, r ^ 1) for r in range(count)])
        place = (far + outer - step) % outer
        out = lax.dynamic_update_slice(out, held[None, None], (place, near) + zeros)
        out = lax.dynamic_update_slice(out, other[None, None], (place, 1 - near) + zeros)
    return out.reshape((count,) + shard.shape)


def gather_tp(rows):
    me = lax.axis_index("tp")
    high, low = me // 2, me % 2
    across = tp_permute(rows, 2)
    pair = jnp.where(high == 0, jnp.stack([rows, across]), jnp.stack([across, rows]))
    twin = tp_permute(pair, 1)
    whole = jnp.where(low == 0, jnp.stack([pair, twin], 1), jnp.stack([twin, pair], 1))
    return whole.reshape((4,) + rows.shape)


def scatter_tp(parts):
    me = lax.axis_index("tp")
    high, low = me // 2, me % 2
    rows, width = parts.shape
    parts = parts.reshape(2, 2, rows // 4, width)
    twin = tp_permute(lax.dynamic_index_in_dim(parts, 1 - low, 1, keepdims=False), 1)
    kept = lax.dynamic_index_in_dim(parts, low, 1, keepdims=False).astype(jnp.float32)
    pair = kept + twin.astype(jnp.float32)
    away = lax.dynamic_index_in_dim(pair, 1 - high, 0, keepdims=False).astype(jnp.bfloat16)
    stay = lax.dynamic_index_in_dim(pair, high, 0, keepdims=False)
    return stay + tp_permute(away, 2).astype(jnp.float32)


def local(
    hidden_in,
    lengths,
    attn_gain,
    mlp_gain,
    q_master,
    k_master,
    trainer_value_weight,
    o_master,
    gate_master,
    up_master,
    down_master,
):
    tp_count = lax.axis_size("tp")
    req_count = lax.axis_size("req")
    tensor_shard_index = lax.axis_index("tp")
    half = jnp.bfloat16
    shard_rows = q_master.shape[0]
    q_cols = q_master.shape[1] // tp_count
    kv_cols = k_master.shape[1]
    ff_cols = gate_master.shape[1] // tp_count
    down_rows = down_master.shape[0]

    q_parts = q_master.reshape(shard_rows, tp_count, q_cols).transpose(1, 0, 2)
    kv_parts = jnp.broadcast_to(
        jnp.concatenate([k_master, trainer_value_weight], axis=1)[None],
        (tp_count, shard_rows, 2 * kv_cols),
    )
    first_pack = jnp.concatenate([q_parts, kv_parts], axis=2).astype(half)
    first_pack = first_pack.reshape(tp_count * shard_rows, q_cols + 2 * kv_cols)
    first_pack = lax.all_to_all(first_pack, "tp", 0, 0, tiled=True)
    first_full = gather_req(first_pack).reshape(-1, q_cols + 2 * kv_cols)

    def ff_parts(master):
        return (
            master.astype(half)
            .reshape(shard_rows, req_count, tp_count, down_rows)
            .transpose(2, 0, 1, 3)
            .reshape(tp_count * shard_rows, ff_cols)
        )

    second_pack = jnp.concatenate([ff_parts(gate_master), ff_parts(up_master)], axis=1)
    second_pack = lax.all_to_all(second_pack, "tp", 0, 0, tiled=True)
    first_full, second_pack, o_own, down_own = lax.optimization_barrier(
        (first_full, second_pack, o_master.astype(half), down_master.astype(half))
    )
    o_full = gather_tp(gather_req(o_own)).transpose(1, 0, 2, 3).reshape(-1, o_own.shape[1])
    second_full = gather_req(second_pack).reshape(-1, 2 * ff_cols)
    down_weight = gather_req(down_own).reshape(ff_cols, down_own.shape[1])

    query_weight = first_full[:, :q_cols]
    key_weight = first_full[:, q_cols : q_cols + kv_cols]
    value_weight = first_full[:, q_cols + kv_cols :]
    gate_weight = second_full[:, :ff_cols]
    up_weight = second_full[:, ff_cols:]
    prompt_batch, sequence_length, model_width = hidden_in.shape
    tok_rows = prompt_batch * sequence_length
    flat_rows = hidden_in.reshape(tok_rows, model_width).astype(jnp.float32)
    normalized_input = rms_norm(flat_rows, attn_gain)
    local_heads = query_weight.shape[1] // HEAD_DIM
    queries = jnp.dot(normalized_input, query_weight, preferred_element_type=jnp.float32).reshape(
        prompt_batch, sequence_length, local_heads, HEAD_DIM
    )
    key_rows = jnp.dot(normalized_input, key_weight, preferred_element_type=jnp.float32).reshape(
        prompt_batch, sequence_length, KEY_VALUE_HEADS, HEAD_DIM
    )
    value_rows = jnp.dot(
        normalized_input, value_weight, preferred_element_type=jnp.float32
    ).reshape(prompt_batch, sequence_length, KEY_VALUE_HEADS, HEAD_DIM)
    cosine_table, sine_table = rope_tables(sequence_length, HEAD_DIM)
    q_rot = rotate(queries, cosine_table, sine_table).astype(jnp.bfloat16)
    rotated_keys = rotate(key_rows, cosine_table, sine_table).astype(jnp.bfloat16)
    value_halves = value_rows.astype(jnp.bfloat16)
    kv_cache = jnp.concatenate(
        [
            rotated_keys.reshape(prompt_batch, sequence_length, KEY_VALUE_HEADS * HEAD_DIM),
            value_halves.reshape(prompt_batch, sequence_length, KEY_VALUE_HEADS * HEAD_DIM),
        ],
        axis=2,
    )
    owner_shards = (
        tensor_shard_index * local_heads + jnp.arange(local_heads, dtype=jnp.int32)
    ) // (QUERY_HEADS // KEY_VALUE_HEADS)
    selector_mask = (
        owner_shards[:, None] == jnp.arange(KEY_VALUE_HEADS, dtype=jnp.int32)[None, :]
    ).astype(jnp.bfloat16)
    k_local = jnp.einsum(
        "pshd,gh->psgd", rotated_keys, selector_mask, preferred_element_type=jnp.float32
    ).astype(jnp.bfloat16)
    v_local = jnp.einsum(
        "pshd,gh->psgd", value_halves, selector_mask, preferred_element_type=jnp.float32
    ).astype(jnp.bfloat16)
    scores = jnp.einsum(
        "pqhd,pkhd->phqk", q_rot, k_local, preferred_element_type=jnp.float32
    ) / math.sqrt(HEAD_DIM)
    row_index = jnp.arange(sequence_length, dtype=jnp.int32)[:, None]
    col_index = jnp.arange(sequence_length, dtype=jnp.int32)[None, :]
    allowed = (col_index <= row_index)[None, None] & (
        col_index[None, None] < lengths[:, None, None, None]
    )
    scores = jnp.where(allowed, scores, -1e30)
    highest = jnp.max(scores, axis=-1, keepdims=True)
    expo = jnp.exp(scores - highest)
    weight_table = (expo / jnp.sum(expo, axis=-1, keepdims=True)).astype(jnp.bfloat16)
    attended = (
        jnp.einsum("phqk,pkhd->pqhd", weight_table, v_local, preferred_element_type=jnp.float32)
        .astype(jnp.bfloat16)
        .reshape(tok_rows, local_heads * HEAD_DIM)
    )
    own_rows = tok_rows // tp_count
    attended_rows = lax.all_to_all(attended, "tp", 0, 1, tiled=True)
    own_hidden = lax.dynamic_slice_in_dim(flat_rows, tensor_shard_index * own_rows, own_rows, 0)
    middle = own_hidden + jnp.dot(attended_rows, o_full, preferred_element_type=jnp.float32)
    normed_rows = gather_tp(rms_norm(middle, mlp_gain)).reshape(tok_rows, model_width)
    gate_val = jnp.dot(normed_rows, gate_weight, preferred_element_type=jnp.float32)
    up_val = jnp.dot(normed_rows, up_weight, preferred_element_type=jnp.float32)
    hidden_ff = (jax.nn.silu(gate_val) * up_val).astype(jnp.bfloat16)
    ffn_rows = scatter_tp(
        jnp.dot(hidden_ff, down_weight, preferred_element_type=jnp.float32).astype(jnp.bfloat16)
    )
    result = gather_tp((middle + ffn_rows).astype(jnp.bfloat16))
    return (result.reshape(prompt_batch, sequence_length, model_width), kv_cache)


def solution(mesh):
    placed = (
        P("req", None, None),
        P("req"),
        P(),
        P(),
        P(("req", "tp"), None),
        P(("req", "tp"), None),
        P(("req", "tp"), None),
        P(("req", "tp"), None),
        P(("req", "tp"), None),
        P(("req", "tp"), None),
        P(("req", "tp"), None),
    )
    return jax.shard_map(
        local,
        mesh=mesh,
        in_specs=placed,
        out_specs=(P("req", None, None), P("req", None, None)),
        check_vma=False,
    )
```

```python
import math

import jax
import jax.numpy as jnp
from jax import lax
from jax.sharding import PartitionSpec as P

QUERY_HEADS = 20
KEY_VALUE_HEADS = 5
HEAD_DIM = 64


def rms_norm(field, gain_vec):
    scale = lax.rsqrt(jnp.mean(field * field, axis=-1, keepdims=True) + 1e-05)
    return (field * scale * gain_vec).astype(jnp.bfloat16)


def rope_tables(sequence_length, head_size):
    half_width = head_size // 2
    positions = jnp.arange(sequence_length, dtype=jnp.float32)[:, None]
    frequency = jnp.exp(
        -math.log(10000.0) * (2.0 * jnp.arange(half_width, dtype=jnp.float32) / head_size)
    )
    angles = positions * frequency[None, :]
    return (jnp.cos(angles), jnp.sin(angles))


def rotate(field, cosine_table, sine_table):
    half_width = field.shape[-1] // 2
    first_half = field[..., :half_width]
    second_half = field[..., half_width:]
    cos_b = cosine_table[:, None, :]
    sin_b = sine_table[:, None, :]
    return jnp.concatenate(
        [first_half * cos_b - second_half * sin_b, second_half * cos_b + first_half * sin_b],
        axis=-1,
    )


def tp_permute(field, flip):
    return lax.ppermute(field, "tp", [(s, s ^ flip) for s in range(lax.axis_size("tp"))])


def gather_far(shard):
    count = lax.axis_size("req")
    held = [shard]
    for step in range(2, count, 2):
        pairs = [(r, (r + step) % count) for r in range(count)]
        held.append(lax.ppermute(shard, "req", pairs))
    return held


def gather_near(held):
    count = lax.axis_size("req")
    outer = len(held)
    shape = held[0].shape
    me = lax.axis_index("req")
    far, near = me // 2, me % 2
    out = jnp.zeros((outer, 2) + shape, held[0].dtype)
    zeros = (0,) * len(shape)
    swapped = [lax.ppermute(mine, "req", [(r, r ^ 1) for r in range(count)]) for mine in held]
    for step, (mine, other) in enumerate(zip(held, swapped)):
        place = (far + outer - step) % outer
        out = lax.dynamic_update_slice(out, mine[None, None], (place, near) + zeros)
        out = lax.dynamic_update_slice(out, other[None, None], (place, 1 - near) + zeros)
    return out.reshape((count,) + shape)


def tie(*fields):
    return lax.optimization_barrier(fields)


def gather_tp(rows):
    me = lax.axis_index("tp")
    high, low = me // 2, me % 2
    across = tp_permute(rows, 2)
    pair = jnp.where(high == 0, jnp.stack([rows, across]), jnp.stack([across, rows]))
    twin = tp_permute(pair, 1)
    whole = jnp.where(low == 0, jnp.stack([pair, twin], 1), jnp.stack([twin, pair], 1))
    return whole.reshape((4,) + rows.shape)


def scatter_tp(parts):
    me = lax.axis_index("tp")
    high, low = me // 2, me % 2
    rows, width = parts.shape
    parts = parts.reshape(2, 2, rows // 4, width)
    twin = tp_permute(lax.dynamic_index_in_dim(parts, 1 - low, 1, keepdims=False), 1)
    kept = lax.dynamic_index_in_dim(parts, low, 1, keepdims=False).astype(jnp.float32)
    pair = kept + twin.astype(jnp.float32)
    away = lax.dynamic_index_in_dim(pair, 1 - high, 0, keepdims=False).astype(jnp.bfloat16)
    stay = lax.dynamic_index_in_dim(pair, high, 0, keepdims=False)
    return stay + tp_permute(away, 2).astype(jnp.float32)


def local(
    hidden_in,
    lengths,
    attn_gain,
    mlp_gain,
    q_master,
    k_master,
    trainer_value_weight,
    o_master,
    gate_master,
    up_master,
    down_master,
):
    tp_count = lax.axis_size("tp")
    req_count = lax.axis_size("req")
    tensor_shard_index = lax.axis_index("tp")
    half = jnp.bfloat16
    shard_rows = q_master.shape[0]
    q_cols = q_master.shape[1] // tp_count
    kv_cols = k_master.shape[1]
    ff_cols = gate_master.shape[1] // tp_count
    down_rows = down_master.shape[0]

    q_parts = q_master.reshape(shard_rows, tp_count, q_cols).transpose(1, 0, 2)
    kv_parts = jnp.broadcast_to(
        jnp.concatenate([k_master, trainer_value_weight], axis=1)[None],
        (tp_count, shard_rows, 2 * kv_cols),
    )
    first_pack = jnp.concatenate([q_parts, kv_parts], axis=2).astype(half)
    first_pack = first_pack.reshape(tp_count * shard_rows, q_cols + 2 * kv_cols)
    first_pack = lax.all_to_all(first_pack, "tp", 0, 0, tiled=True)
    first_pack, gate_master, up_master, o_master, down_master = tie(
        first_pack, gate_master, up_master, o_master, down_master
    )
    first_far = gather_far(first_pack)
    third_pack = jnp.concatenate([o_master, down_master]).astype(half)
    first_far, third_pack = tie(first_far, third_pack)
    third_far = gather_far(third_pack)
    first_full = gather_near(first_far).reshape(-1, q_cols + 2 * kv_cols)

    def ff_parts(master):
        return (
            master.astype(half)
            .reshape(shard_rows, req_count, tp_count, down_rows)
            .transpose(2, 0, 1, 3)
            .reshape(tp_count * shard_rows, ff_cols)
        )

    second_pack = jnp.concatenate([ff_parts(gate_master), ff_parts(up_master)], axis=1)
    second_pack = lax.all_to_all(second_pack, "tp", 0, 0, tiled=True)
    query_weight = first_full[:, :q_cols]
    key_weight = first_full[:, q_cols : q_cols + kv_cols]
    value_weight = first_full[:, q_cols + kv_cols :]
    prompt_batch, sequence_length, model_width = hidden_in.shape
    tok_rows = prompt_batch * sequence_length
    flat_rows = hidden_in.reshape(tok_rows, model_width).astype(jnp.float32)
    normalized_input = rms_norm(flat_rows, attn_gain)
    local_heads = query_weight.shape[1] // HEAD_DIM
    queries = jnp.dot(normalized_input, query_weight, preferred_element_type=jnp.float32).reshape(
        prompt_batch, sequence_length, local_heads, HEAD_DIM
    )
    key_rows = jnp.dot(normalized_input, key_weight, preferred_element_type=jnp.float32).reshape(
        prompt_batch, sequence_length, KEY_VALUE_HEADS, HEAD_DIM
    )
    value_rows = jnp.dot(
        normalized_input, value_weight, preferred_element_type=jnp.float32
    ).reshape(prompt_batch, sequence_length, KEY_VALUE_HEADS, HEAD_DIM)
    queries, key_rows, value_rows, third_far, second_pack = tie(
        queries, key_rows, value_rows, third_far, second_pack
    )
    second_far = gather_far(second_pack)
    third_full = gather_near(third_far)
    cosine_table, sine_table = rope_tables(sequence_length, HEAD_DIM)
    q_rot = rotate(queries, cosine_table, sine_table).astype(jnp.bfloat16)
    rotated_keys = rotate(key_rows, cosine_table, sine_table).astype(jnp.bfloat16)
    value_halves = value_rows.astype(jnp.bfloat16)
    kv_cache = jnp.concatenate(
        [
            rotated_keys.reshape(prompt_batch, sequence_length, KEY_VALUE_HEADS * HEAD_DIM),
            value_halves.reshape(prompt_batch, sequence_length, KEY_VALUE_HEADS * HEAD_DIM),
        ],
        axis=2,
    )
    owner_shards = (
        tensor_shard_index * local_heads + jnp.arange(local_heads, dtype=jnp.int32)
    ) // (QUERY_HEADS // KEY_VALUE_HEADS)
    selector_mask = (
        owner_shards[:, None] == jnp.arange(KEY_VALUE_HEADS, dtype=jnp.int32)[None, :]
    ).astype(jnp.bfloat16)
    k_local = jnp.einsum(
        "pshd,gh->psgd", rotated_keys, selector_mask, preferred_element_type=jnp.float32
    ).astype(jnp.bfloat16)
    v_local = jnp.einsum(
        "pshd,gh->psgd", value_halves, selector_mask, preferred_element_type=jnp.float32
    ).astype(jnp.bfloat16)
    scores = jnp.einsum(
        "pqhd,pkhd->phqk", q_rot, k_local, preferred_element_type=jnp.float32
    ) / math.sqrt(HEAD_DIM)
    row_index = jnp.arange(sequence_length, dtype=jnp.int32)[:, None]
    col_index = jnp.arange(sequence_length, dtype=jnp.int32)[None, :]
    allowed = (col_index <= row_index)[None, None] & (
        col_index[None, None] < lengths[:, None, None, None]
    )
    scores = jnp.where(allowed, scores, -1e30)
    highest = jnp.max(scores, axis=-1, keepdims=True)
    expo = jnp.exp(scores - highest)
    weight_table = (expo / jnp.sum(expo, axis=-1, keepdims=True)).astype(jnp.bfloat16)
    attended = (
        jnp.einsum("phqk,pkhd->pqhd", weight_table, v_local, preferred_element_type=jnp.float32)
        .astype(jnp.bfloat16)
        .reshape(tok_rows, local_heads * HEAD_DIM)
    )
    attended, second_far, third_full = tie(attended, second_far, third_full)
    second_full = gather_near(second_far).reshape(-1, 2 * ff_cols)
    o_own, down_weight = third_full[:, :shard_rows], third_full[:, shard_rows:]
    down_weight = down_weight.reshape(ff_cols, model_width)
    o_full = gather_tp(o_own).transpose(1, 0, 2, 3).reshape(-1, model_width)
    gate_weight = second_full[:, :ff_cols]
    up_weight = second_full[:, ff_cols:]
    own_rows = tok_rows // tp_count
    attended_rows = lax.all_to_all(attended, "tp", 0, 1, tiled=True)
    own_hidden = lax.dynamic_slice_in_dim(flat_rows, tensor_shard_index * own_rows, own_rows, 0)
    middle = own_hidden + jnp.dot(attended_rows, o_full, preferred_element_type=jnp.float32)
    normed_rows = gather_tp(rms_norm(middle, mlp_gain))
    results = []
    for chunk in range(2):
        part = slice(chunk * own_rows // 2, (chunk + 1) * own_rows // 2)
        rows = normed_rows[:, part].reshape(tok_rows // 2, model_width)
        gate_val = jnp.dot(rows, gate_weight, preferred_element_type=jnp.float32)
        up_val = jnp.dot(rows, up_weight, preferred_element_type=jnp.float32)
        hidden_ff = (jax.nn.silu(gate_val) * up_val).astype(jnp.bfloat16)
        sums = scatter_tp(
            jnp.dot(hidden_ff, down_weight, preferred_element_type=jnp.float32).astype(
                jnp.bfloat16
            )
        )
        results.append(gather_tp((middle[part] + sums).astype(jnp.bfloat16)))
    result = jnp.concatenate(results, axis=1)
    return (result.reshape(prompt_batch, sequence_length, model_width), kv_cache)


def solution(mesh):
    placed = (
        P("req", None, None),
        P("req"),
        P(),
        P(),
        P(("req", "tp"), None),
        P(("req", "tp"), None),
        P(("req", "tp"), None),
        P(("req", "tp"), None),
        P(("req", "tp"), None),
        P(("req", "tp"), None),
        P(("req", "tp"), None),
    )
    return jax.shard_map(
        local,
        mesh=mesh,
        in_specs=placed,
        out_specs=(P("req", None, None), P("req", None, None)),
        check_vma=False,
    )
```

```python
import math

import jax
import jax.numpy as jnp
from jax import lax
from jax.sharding import PartitionSpec as P

QUERY_HEADS = 20
KEY_VALUE_HEADS = 5
HEAD_DIM = 64


def rms_norm(field, gain_vec):
    scale = lax.rsqrt(jnp.mean(field * field, axis=-1, keepdims=True) + 1e-05)
    return (field * scale * gain_vec).astype(jnp.bfloat16)


def rope_tables(sequence_length, head_size):
    half_width = head_size // 2
    positions = jnp.arange(sequence_length, dtype=jnp.float32)[:, None]
    frequency = jnp.exp(
        -math.log(10000.0) * (2.0 * jnp.arange(half_width, dtype=jnp.float32) / head_size)
    )
    angles = positions * frequency[None, :]
    return (jnp.cos(angles), jnp.sin(angles))


def rotate(field, cosine_table, sine_table):
    half_width = field.shape[-1] // 2
    first_half = field[..., :half_width]
    second_half = field[..., half_width:]
    cos_b = cosine_table[:, None, :]
    sin_b = sine_table[:, None, :]
    return jnp.concatenate(
        [first_half * cos_b - second_half * sin_b, second_half * cos_b + first_half * sin_b],
        axis=-1,
    )


def tp_permute(field, flip):
    return lax.ppermute(field, "tp", [(s, s ^ flip) for s in range(lax.axis_size("tp"))])


def gather_far(shard):
    count = lax.axis_size("req")
    held = [shard]
    for step in range(2, count, 2):
        pairs = [(r, (r + step) % count) for r in range(count)]
        held.append(lax.ppermute(shard, "req", pairs))
    return held


def swap_near(held):
    count = lax.axis_size("req")
    return [lax.ppermute(mine, "req", [(r, r ^ 1) for r in range(count)]) for mine in held]


def gather_near(held, swapped):
    count = lax.axis_size("req")
    outer = len(held)
    shape = held[0].shape
    me = lax.axis_index("req")
    far, near = me // 2, me % 2
    out = jnp.zeros((outer, 2) + shape, held[0].dtype)
    zeros = (0,) * len(shape)
    for step, (mine, other) in enumerate(zip(held, swapped)):
        place = (far + outer - step) % outer
        out = lax.dynamic_update_slice(out, mine[None, None], (place, near) + zeros)
        out = lax.dynamic_update_slice(out, other[None, None], (place, 1 - near) + zeros)
    return out.reshape((count,) + shape)


def tie(*fields):
    return lax.optimization_barrier(fields)


def gather_tp(rows):
    me = lax.axis_index("tp")
    high, low = me // 2, me % 2
    across = tp_permute(rows, 2)
    pair = jnp.where(high == 0, jnp.stack([rows, across]), jnp.stack([across, rows]))
    twin = tp_permute(pair, 1)
    whole = jnp.where(low == 0, jnp.stack([pair, twin], 1), jnp.stack([twin, pair], 1))
    return whole.reshape((4,) + rows.shape)


def scatter_tp(parts):
    me = lax.axis_index("tp")
    high, low = me // 2, me % 2
    rows, width = parts.shape
    parts = parts.reshape(2, 2, rows // 4, width)
    twin = tp_permute(lax.dynamic_index_in_dim(parts, 1 - low, 1, keepdims=False), 1)
    kept = lax.dynamic_index_in_dim(parts, low, 1, keepdims=False).astype(jnp.float32)
    pair = kept + twin.astype(jnp.float32)
    away = lax.dynamic_index_in_dim(pair, 1 - high, 0, keepdims=False).astype(jnp.bfloat16)
    stay = lax.dynamic_index_in_dim(pair, high, 0, keepdims=False)
    return stay + tp_permute(away, 2).astype(jnp.float32)


def local(
    hidden_in,
    lengths,
    attn_gain,
    mlp_gain,
    q_master,
    k_master,
    trainer_value_weight,
    o_master,
    gate_master,
    up_master,
    down_master,
):
    tp_count = lax.axis_size("tp")
    req_count = lax.axis_size("req")
    tensor_shard_index = lax.axis_index("tp")
    half = jnp.bfloat16
    shard_rows = q_master.shape[0]
    q_cols = q_master.shape[1] // tp_count
    kv_cols = k_master.shape[1]
    ff_cols = gate_master.shape[1] // tp_count
    down_rows = down_master.shape[0]

    q_parts = q_master.reshape(shard_rows, tp_count, q_cols).transpose(1, 0, 2)
    kv_parts = jnp.broadcast_to(
        jnp.concatenate([k_master, trainer_value_weight], axis=1)[None],
        (tp_count, shard_rows, 2 * kv_cols),
    )
    first_pack = jnp.concatenate([q_parts, kv_parts], axis=2).astype(half)
    first_pack = first_pack.reshape(tp_count * shard_rows, q_cols + 2 * kv_cols)
    first_pack = lax.all_to_all(first_pack, "tp", 0, 0, tiled=True)
    first_pack, gate_master, up_master, o_master, down_master = tie(
        first_pack, gate_master, up_master, o_master, down_master
    )
    first_far = gather_far(first_pack)
    third_pack = jnp.concatenate([o_master, down_master]).astype(half)
    first_far, third_pack = tie(first_far, third_pack)
    third_far = gather_far(third_pack)
    first_full = gather_near(first_far, swap_near(first_far)).reshape(-1, q_cols + 2 * kv_cols)

    def ff_parts(master):
        return (
            master.astype(half)
            .reshape(shard_rows, req_count, tp_count, down_rows)
            .transpose(2, 0, 1, 3)
            .reshape(tp_count * shard_rows, ff_cols)
        )

    second_pack = jnp.concatenate([ff_parts(gate_master), ff_parts(up_master)], axis=1)
    second_pack = lax.all_to_all(second_pack, "tp", 0, 0, tiled=True)
    query_weight = first_full[:, :q_cols]
    key_weight = first_full[:, q_cols : q_cols + kv_cols]
    value_weight = first_full[:, q_cols + kv_cols :]
    prompt_batch, sequence_length, model_width = hidden_in.shape
    tok_rows = prompt_batch * sequence_length
    flat_rows = hidden_in.reshape(tok_rows, model_width).astype(jnp.float32)
    normalized_input = rms_norm(flat_rows, attn_gain)
    local_heads = query_weight.shape[1] // HEAD_DIM
    queries = jnp.dot(normalized_input, query_weight, preferred_element_type=jnp.float32).reshape(
        prompt_batch, sequence_length, local_heads, HEAD_DIM
    )
    key_rows = jnp.dot(normalized_input, key_weight, preferred_element_type=jnp.float32).reshape(
        prompt_batch, sequence_length, KEY_VALUE_HEADS, HEAD_DIM
    )
    value_rows = jnp.dot(
        normalized_input, value_weight, preferred_element_type=jnp.float32
    ).reshape(prompt_batch, sequence_length, KEY_VALUE_HEADS, HEAD_DIM)
    queries, key_rows, value_rows, third_far, second_pack = tie(
        queries, key_rows, value_rows, third_far, second_pack
    )
    second_far = gather_far(second_pack)
    third_swapped = swap_near(third_far)
    cosine_table, sine_table = rope_tables(sequence_length, HEAD_DIM)
    q_rot = rotate(queries, cosine_table, sine_table).astype(jnp.bfloat16)
    rotated_keys = rotate(key_rows, cosine_table, sine_table).astype(jnp.bfloat16)
    value_halves = value_rows.astype(jnp.bfloat16)
    kv_cache = jnp.concatenate(
        [
            rotated_keys.reshape(prompt_batch, sequence_length, KEY_VALUE_HEADS * HEAD_DIM),
            value_halves.reshape(prompt_batch, sequence_length, KEY_VALUE_HEADS * HEAD_DIM),
        ],
        axis=2,
    )
    owner_shards = (
        tensor_shard_index * local_heads + jnp.arange(local_heads, dtype=jnp.int32)
    ) // (QUERY_HEADS // KEY_VALUE_HEADS)
    selector_mask = (
        owner_shards[:, None] == jnp.arange(KEY_VALUE_HEADS, dtype=jnp.int32)[None, :]
    ).astype(jnp.bfloat16)
    k_local = jnp.einsum(
        "pshd,gh->psgd", rotated_keys, selector_mask, preferred_element_type=jnp.float32
    ).astype(jnp.bfloat16)
    v_local = jnp.einsum(
        "pshd,gh->psgd", value_halves, selector_mask, preferred_element_type=jnp.float32
    ).astype(jnp.bfloat16)
    ahead = len(third_swapped) // 2
    v_local, early = tie(v_local, third_swapped[:ahead])
    third_full = gather_near(third_far, early + third_swapped[ahead:])
    scores = jnp.einsum(
        "pqhd,pkhd->phqk", q_rot, k_local, preferred_element_type=jnp.float32
    ) / math.sqrt(HEAD_DIM)
    row_index = jnp.arange(sequence_length, dtype=jnp.int32)[:, None]
    col_index = jnp.arange(sequence_length, dtype=jnp.int32)[None, :]
    allowed = (col_index <= row_index)[None, None] & (
        col_index[None, None] < lengths[:, None, None, None]
    )
    scores = jnp.where(allowed, scores, -1e30)
    highest = jnp.max(scores, axis=-1, keepdims=True)
    expo = jnp.exp(scores - highest)
    weight_table = (expo / jnp.sum(expo, axis=-1, keepdims=True)).astype(jnp.bfloat16)
    attended = (
        jnp.einsum("phqk,pkhd->pqhd", weight_table, v_local, preferred_element_type=jnp.float32)
        .astype(jnp.bfloat16)
        .reshape(tok_rows, local_heads * HEAD_DIM)
    )
    attended, second_far, third_full = tie(attended, second_far, third_full)
    second_full = gather_near(second_far, swap_near(second_far)).reshape(-1, 2 * ff_cols)
    o_own, down_weight = third_full[:, :shard_rows], third_full[:, shard_rows:]
    down_weight = down_weight.reshape(ff_cols, model_width)
    o_full = gather_tp(o_own).transpose(1, 0, 2, 3).reshape(-1, model_width)
    gate_weight = second_full[:, :ff_cols]
    up_weight = second_full[:, ff_cols:]
    own_rows = tok_rows // tp_count
    attended_rows = lax.all_to_all(attended, "tp", 0, 1, tiled=True)
    own_hidden = lax.dynamic_slice_in_dim(flat_rows, tensor_shard_index * own_rows, own_rows, 0)
    middle = own_hidden + jnp.dot(attended_rows, o_full, preferred_element_type=jnp.float32)
    normed_rows = gather_tp(rms_norm(middle, mlp_gain))
    results = []
    for chunk in range(2):
        part = slice(chunk * own_rows // 2, (chunk + 1) * own_rows // 2)
        rows = normed_rows[:, part].reshape(tok_rows // 2, model_width)
        gate_val = jnp.dot(rows, gate_weight, preferred_element_type=jnp.float32)
        up_val = jnp.dot(rows, up_weight, preferred_element_type=jnp.float32)
        hidden_ff = (jax.nn.silu(gate_val) * up_val).astype(jnp.bfloat16)
        sums = scatter_tp(
            jnp.dot(hidden_ff, down_weight, preferred_element_type=jnp.float32).astype(
                jnp.bfloat16
            )
        )
        results.append(gather_tp((middle[part] + sums).astype(jnp.bfloat16)))
    result = jnp.concatenate(results, axis=1)
    return (result.reshape(prompt_batch, sequence_length, model_width), kv_cache)


def solution(mesh):
    placed = (
        P("req", None, None),
        P("req"),
        P(),
        P(),
        P(("req", "tp"), None),
        P(("req", "tp"), None),
        P(("req", "tp"), None),
        P(("req", "tp"), None),
        P(("req", "tp"), None),
        P(("req", "tp"), None),
        P(("req", "tp"), None),
    )
    return jax.shard_map(
        local,
        mesh=mesh,
        in_specs=placed,
        out_specs=(P("req", None, None), P("req", None, None)),
        check_vma=False,
    )
```
